32 devices in a mesh: dp: 4 (over z), ctx: 4 (over y, x), tensor: 2 (over core).
Axes of the slice: x: 2, y: 2, z: 4, core: 2. Of those that a mesh axis runs over, the one named last changes fastest.
Arguments:
- tokens: bfloat16 [16, 256, 384], P('dp', 'ctx'), may hold values from -6 to 6
- cond: bfloat16 [16, 384], P('dp'), may hold values from -6 to 6
- latent_count: int32 [4], P('dp'), may hold values from 2 to 4, as said below
- cotangent: bfloat16 [16, 256, 384], P('dp', 'ctx'), may hold values from -6 to 6
- ada_w: bfloat16 [1, 384, 2304], P(None, 'dp'), may hold values from -0.3125 to 0.3125
- ada_b: bfloat16 [1, 2304], replicated, may hold values from -3 to 3
- qkv_w: bfloat16 [1, 384, 3, 6, 64], P(None, 'dp', None, 'tensor'), may hold values from -0.3125 to 0.3125
- qv_b: bfloat16 [1, 2, 6, 64], P(None, None, 'tensor'), may hold values from -1.1953125 to 1.1953125
- out_w: bfloat16 [1, 6, 64, 384], P(None, 'tensor', None, 'dp'), may hold values from -1.25 to 1.25
- out_b: bfloat16 [1, 384], replicated, may hold values from -1.1953125 to 1.1953125
- fc1_w: bfloat16 [1, 384, 1536], P(None, 'dp', 'tensor'), may hold values from -0.3125 to 0.3125
- fc1_b: bfloat16 [1, 1536], P(None, 'tensor'), may hold values from -1.796875 to 1.796875
- fc2_w: bfloat16 [1, 1536, 384], P(None, 'tensor', 'dp'), may hold values from -0.15625 to 0.15625
- fc2_b: bfloat16 [1, 384], replicated, may hold values from -1.1953125 to 1.1953125
Outputs:
- mixed: bfloat16 [16, 256, 384], P('dp', 'ctx')
- tokens_grad: float32 [16, 256, 384], P('dp', 'ctx')
- cond_grad: float32 [16, 384], P('dp')
- ada_w_grad: float32 [1, 384, 2304], P(None, 'dp')
- ada_b_grad: float32 [1, 2304], replicated
- qkv_w_grad: float32 [1, 384, 3, 6, 64], P(None, 'dp', None, 'tensor')
- qv_b_grad: float32 [1, 2, 6, 64], P(None, None, 'tensor')
- out_w_grad: float32 [1, 6, 64, 384], P(None, 'tensor', None, 'dp')
- out_b_grad: float32 [1, 384], replicated
- fc1_w_grad: float32 [1, 384, 1536], P(None, 'dp', 'tensor')
- fc1_b_grad: float32 [1, 1536], P(None, 'tensor')
- fc2_w_grad: float32 [1, 1536, 384], P(None, 'tensor', 'dp')
- fc2_b_grad: float32 [1, 384], replicated
The draws below stay inside these ranges and needn't reach their ends.
Inputs may be any that keep to these rules, and one draw needn't show every extreme that they name: `latent_count`: the live latents of an index of dp fill its first slots of 4, the others are empty; in every draw some index holds 4.
All inputs are finite; a program needn't handle non-finite values.
Results may differ from the reference program's by a relative error of at most 0.015.
The reference program's roundings to bfloat16 on the way count: a program that leaves them out, or rounds other values in their place, can miss the bound.
Values may be sent and summed in bfloat16 or wider, within the bound.
A program may use at most 64 MiB of HBM per device.

```python
import math
import jax
import jax.numpy as jnp
from jax import lax

D = 384
H = 6
HD = 64
FF = 1536
SEQ = 256
LAYERS = 1
LAT_DEV = 4
LATENTS = 16
N_DP = 4


def draw_latent_count(key, part):
    key = jax.random.fold_in(key, 7)
    count_key, fullest_key = jax.random.split(key)
    counts = jax.random.randint(count_key, (N_DP,), (LAT_DEV + 1) // 2, LAT_DEV + 1)
    fullest = jax.random.randint(fullest_key, (), 0, N_DP)
    return jnp.where(jnp.arange(N_DP) == fullest, LAT_DEV, counts).astype(jnp.int32)


def level_of(stream_key, dims, cuts, smallest, high):
    gain = 1.0
    for position, blocks in cuts:
        draws = jax.random.uniform(jax.random.fold_in(jax.random.fold_in(stream_key, 6), position), (blocks,), jnp.float32, smallest / len(cuts), high / len(cuts))
        gain = gain * jnp.repeat(jnp.exp(draws), dims[position] // blocks).reshape((-1,) + (1,) * (len(dims) - 1 - position))
    return gain


def bell_draw(rng, shape, width, limit, cuts=(), kind=jnp.bfloat16):
    values = width * jax.random.normal(rng, shape, jnp.float32)
    if cuts:
        values = values * level_of(rng, shape, cuts, -0.22, 0.18)
    return jnp.clip(values, -limit, limit).astype(kind)


def setup_inputs(seed: int = 0) -> dict:
    key_list = jax.random.split(jax.random.key(seed), 15)
    tokens = bell_draw(key_list[0], (LATENTS, SEQ, D), 1.0, 6.0, ((0, 4), (1, 4)))
    cond = bell_draw(key_list[1], (LATENTS, D), 1.0, 6.0, ((0, 4),))
    latent_count = draw_latent_count(jax.random.fold_in(key_list[14], 71), 0)
    cotangent = bell_draw(key_list[3], (LATENTS, SEQ, D), 1.0, 6.0, ((0, 4), (1, 4)))
    ada_w = bell_draw(key_list[4], (LAYERS, D, 6 * D), D ** -0.5, 0.3125, ((1, 4),))
    ada_b = bell_draw(key_list[5], (LAYERS, 6 * D), 0.5, 3.0)
    qkv_w = bell_draw(key_list[6], (LAYERS, D, 3, H, HD), D ** -0.5, 0.3125, ((1, 4), (3, 2)))
    qv_b = bell_draw(key_list[7], (LAYERS, 2, H, HD), 0.2, 1.1953125, ((2, 2),))
    out_w = bell_draw(key_list[8], (LAYERS, H, HD, D), (D * 16 // SEQ) ** -0.5, 1.25, ((1, 2), (3, 4)))
    out_b = bell_draw(key_list[9], (LAYERS, D), 0.2, 1.1953125)
    fc1_w = bell_draw(key_list[10], (LAYERS, D, FF), D ** -0.5, 0.3125, ((1, 4), (2, 2)))
    fc1_b = bell_draw(key_list[11], (LAYERS, FF), 0.3, 1.796875, ((1, 2),))
    fc2_w = bell_draw(key_list[12], (LAYERS, FF, D), FF ** -0.5, 0.15625, ((1, 2), (2, 4)))
    fc2_b = bell_draw(key_list[13], (LAYERS, D), 0.2, 1.1953125)
    return dict(tokens=tokens, cond=cond, latent_count=latent_count, cotangent=cotangent, ada_w=ada_w, ada_b=ada_b, qkv_w=qkv_w, qv_b=qv_b, out_w=out_w, out_b=out_b, fc1_w=fc1_w, fc1_b=fc1_b, fc2_w=fc2_w, fc2_b=fc2_b)


@jax.custom_vjp
def low(v):
    return lax.optimization_barrier(v.astype(jnp.bfloat16)).astype(jnp.float32)

@jax.custom_vjp
def low_back(v):
    return v

def low_keep(v):
    return (low(v), None)

def low_pass(kept, grad):
    return (grad,)

def back_keep(v):
    return (v, None)

def back_low(kept, grad):
    return (low(grad),)
low.defvjp(low_keep, low_pass)
low_back.defvjp(back_keep, back_low)
EPSILON = 1e-06
PRECISE = lax.Precision.HIGHEST

def matmul_exact(left, right):
    return jnp.dot(left, right, precision=PRECISE, preferred_element_type=jnp.float32)

def layer_norm(residual_state):
    row_mean = lax.optimization_barrier(jnp.mean(residual_state, axis=-1, keepdims=True))
    centered = residual_state - row_mean
    return centered * lax.rsqrt(lax.optimization_barrier(jnp.mean(centered * centered, axis=-1, keepdims=True)) + EPSILON)

def attend_block(operands):
    queries, key_rows, value_rows = operands
    scores = jnp.einsum('gqhe,gkhe->ghqk', queries, key_rows, precision=PRECISE) * HD ** (-0.5)
    scores = low_back(scores)
    row_max = lax.optimization_barrier(jnp.max(scores, axis=-1, keepdims=True))
    weights = jnp.exp(scores - row_max)
    row_sum = lax.optimization_barrier(jnp.sum(weights, axis=-1, keepdims=True))
    summed = jnp.einsum('ghqk,gkhe->gqhe', low(weights), value_rows, precision=PRECISE)
    return summed / jnp.transpose(row_sum, (0, 2, 1, 3))

def diffusion_transformer_block(residual_state, activated_conditioning, model_parameters):
    ada_w, ada_b, qkv_w, qv_b, out_w, out_b, fc1_w, fc1_b, fc2_w, fc2_b = model_parameters
    latents, seq_len, model_width = residual_state.shape
    head_count, head_size = (qkv_w.shape[2], qkv_w.shape[3])
    row_count = latents * seq_len
    modulation = (matmul_exact(activated_conditioning, ada_w) + ada_b).reshape(latents, 6, model_width)
    shift_attn, scale_attn, gate_attn, shift_mlp, scale_mlp, gate_mlp = [modulation[:, slot_index][:, None, :] for slot_index in range(6)]
    attn_in = low(layer_norm(residual_state) * (1.0 + scale_attn) + shift_attn)
    projected = matmul_exact(attn_in.reshape(row_count, model_width), qkv_w.reshape(model_width, 3 * head_count * head_size))
    projected = projected.reshape(latents, seq_len, 3, head_count, head_size)
    bias_rows = jnp.stack([qv_b[0], jnp.zeros_like(qv_b[0]), qv_b[1]])
    qkv_rows = low(low_back(projected + bias_rows))
    group_size = math.gcd(latents, 16)
    shaped = tuple((qkv_rows[:, :, which].reshape(latents // group_size, group_size, seq_len, head_count, head_size) for which in range(3)))
    attended = lax.map(jax.checkpoint(attend_block), shaped)
    attended = low(low_back(attended.reshape(row_count, head_count * head_size)))
    branch_attn = low_back(matmul_exact(attended, out_w.reshape(head_count * head_size, model_width)) + out_b)
    middle = residual_state + gate_attn * branch_attn.reshape(latents, seq_len, model_width)
    mlp_in = low(layer_norm(middle) * (1.0 + scale_mlp) + shift_mlp)
    hidden_pre = low_back(matmul_exact(mlp_in.reshape(row_count, model_width), fc1_w) + fc1_b)
    hidden_act = low(jax.nn.gelu(hidden_pre, approximate=True))
    branch_mlp = low_back(matmul_exact(hidden_act, fc2_w) + fc2_b)
    return middle + gate_mlp * branch_mlp.reshape(latents, seq_len, model_width)

def reference(tokens, cond, latent_count, cotangent, ada_w, ada_b, qkv_w, qv_b, out_w, out_b, fc1_w, fc1_b, fc2_w, fc2_b):
    owner = jnp.arange(LATENTS, dtype=jnp.int32) // LAT_DEV
    slot_number = jnp.arange(LATENTS, dtype=jnp.int32) % LAT_DEV
    live_mask = (slot_number < latent_count[owner]).astype(jnp.float32)[:, None, None]
    model_parameters = tuple((weight.astype(jnp.float32) for weight in (ada_w, ada_b, qkv_w, qv_b, out_w, out_b, fc1_w, fc1_b, fc2_w, fc2_b)))

    def forward(residual_state, cond_rows, *layer_parameters):
        activated_conditioning = low(jax.nn.silu(cond_rows))
        for layer_position in range(LAYERS):
            residual_state = jax.checkpoint(diffusion_transformer_block)(residual_state, activated_conditioning, tuple((stacked_layers[layer_position] for stacked_layers in layer_parameters)))
        return residual_state * live_mask
    result, pullback = jax.vjp(forward, tokens.astype(jnp.float32), cond.astype(jnp.float32), *model_parameters)
    grads = pullback(cotangent.astype(jnp.float32))
    return (result.astype(jnp.bfloat16), grads[0], grads[1], grads[2], grads[3], grads[4], grads[5], grads[6], grads[7], grads[8], grads[9], grads[10], grads[11])
```

```python
import jax
import jax.numpy as jnp
from jax import lax
from jax.experimental import pallas as pl
from jax.experimental.pallas import tpu as pltpu
from jax.sharding import PartitionSpec as P

HD = 64


EPSILON = 1e-06
PRECISE = lax.Precision.HIGHEST


def layer_norm(residual_state):
    row_mean = jnp.mean(residual_state, axis=-1, keepdims=True)
    centered = residual_state - row_mean
    inv_std = lax.rsqrt(jnp.mean(centered * centered, axis=-1, keepdims=True) + EPSILON)
    return (centered * inv_std, inv_std)


def norm_back(upstream, normed, inv_std):
    first = jnp.mean(upstream, axis=-1, keepdims=True)
    second = jnp.mean(upstream * normed, axis=-1, keepdims=True)
    return inv_std * (upstream - first - normed * second)


def split_six(modulation, model_width):
    shaped = modulation.reshape(modulation.shape[0], 6, model_width)
    return [shaped[:, slot_index][:, None, :] for slot_index in range(6)]


MESH = pl.DeviceIdType.MESH
ANY = pl.BlockSpec(memory_space=pl.ANY)


def peer(axis, step):
    size = lax.axis_size(axis)
    return lax.rem(lax.axis_index(axis) + step, size)


def source(axis, step):
    size = lax.axis_size(axis)
    return lax.rem(lax.axis_index(axis) + size - step, size)


def greet(axes):
    barrier = pltpu.get_barrier_semaphore()
    total = 0
    for axis in axes:
        for step in range(1, lax.axis_size(axis)):
            pl.semaphore_signal(
                barrier, inc=1, device_id={axis: peer(axis, step)}, device_id_type=MESH
            )
            total += 1
    pl.semaphore_wait(barrier, total)


def exchange(collective_id, *items):
    count = len(items)
    axes = sorted({axis for _, axis, _ in items})
    steps_of = [lax.axis_size(axis) - 1 for _, axis, _ in items]
    firsts = [sum(steps_of[:which]) for which in range(count)]
    total = sum(steps_of)

    def body(*refs):
        ins, outs = refs[:count], refs[count : 2 * count]
        send_sem, recv_sem, local_sem = refs[2 * count :]
        greet(axes)
        copies = []
        for which, (kind, axis, _) in enumerate(items):
            me = lax.axis_index(axis)
            for step in range(1, lax.axis_size(axis)):
                to = peer(axis, step)
                copy = pltpu.make_async_remote_copy(
                    src_ref=ins[which] if kind == "gather" else ins[which].at[to],
                    dst_ref=outs[which].at[me],
                    send_sem=send_sem.at[firsts[which] + step - 1],
                    recv_sem=recv_sem.at[firsts[which] + step - 1],
                    device_id={axis: to},
                    device_id_type=MESH,
                )
                copy.start()
                copies.append(copy)
        for which, (kind, axis, _) in enumerate(items):
            me = lax.axis_index(axis)
            copy = pltpu.make_async_copy(
                ins[which] if kind == "gather" else ins[which].at[me],
                outs[which].at[me],
                local_sem.at[which],
            )
            copy.start()
            copies.append(copy)
        for copy in copies:
            copy.wait()

    shapes = [
        jax.ShapeDtypeStruct(
            (lax.axis_size(axis),) + array.shape if kind == "gather" else array.shape, array.dtype
        )
        for kind, axis, array in items
    ]
    return pl.pallas_call(
        body,
        out_shape=shapes,
        in_specs=[ANY] * count,
        out_specs=[ANY] * count,
        scratch_shapes=[
            pltpu.SemaphoreType.DMA((total,)),
            pltpu.SemaphoreType.DMA((total,)),
            pltpu.SemaphoreType.DMA((count,)),
        ],
        compiler_params=pltpu.CompilerParams(collective_id=collective_id, has_side_effects=True),
        name="exchange",
    )(*[array for _, _, array in items])


def gather_weights(collective_id, shard, cond_rows):
    dp_size, ctx_size = lax.axis_size("dp"), lax.axis_size("ctx")
    far, near = dp_size - 1, ctx_size - 1

    def body(x, c, out, c_out, send_a, recv_a, send_b, recv_b, send_c, recv_c, local_sem):
        row, col = lax.axis_index("dp"), lax.axis_index("ctx")
        greet(("dp", "ctx"))
        first, conds, later = [], [], []
        for step in range(1, dp_size):
            target = {"dp": peer("dp", step)}
            copy = pltpu.make_async_remote_copy(
                c, c_out.at[row], send_c.at[step - 1], recv_c.at[step - 1], target, MESH
            )
            copy.start()
            conds.append(copy)
            copy = pltpu.make_async_remote_copy(
                x.at[col], out.at[row, col], send_a.at[step - 1], recv_a.at[step - 1], target, MESH
            )
            copy.start()
            first.append(copy)
        own = pltpu.make_async_copy(x, out.at[row], local_sem.at[0])
        own.start()
        own_cond = pltpu.make_async_copy(c, c_out.at[row], local_sem.at[1])
        own_cond.start()
        for step in range(1, dp_size):
            first[step - 1].wait_recv()
            origin = source("dp", step)
            for hop in range(1, ctx_size):
                where = (step - 1) * near + hop - 1
                copy = pltpu.make_async_remote_copy(
                    out.at[origin, col],
                    out.at[origin, col],
                    send_b.at[where],
                    recv_b.at[where],
                    {"ctx": peer("ctx", hop)},
                    MESH,
                )
                copy.start()
                later.append(copy)
        for copy in first:
            copy.wait_send()
        for copy in conds + later:
            copy.wait()
        own.wait()
        own_cond.wait()

    dma = pltpu.SemaphoreType.DMA
    return pl.pallas_call(
        body,
        out_shape=[
            jax.ShapeDtypeStruct((dp_size,) + shard.shape, shard.dtype),
            jax.ShapeDtypeStruct((dp_size,) + cond_rows.shape, cond_rows.dtype),
        ],
        in_specs=[ANY] * 2,
        out_specs=[ANY] * 2,
        scratch_shapes=[
            dma((far,)),
            dma((far,)),
            dma((far * near,)),
            dma((far * near,)),
            dma((far,)),
            dma((far,)),
            dma((2,)),
        ],
        compiler_params=pltpu.CompilerParams(collective_id=collective_id, has_side_effects=True),
        name="gather_weights",
    )(shard, cond_rows)


def tensor_total(collective_id, partial_rows):
    return jnp.sum(exchange(collective_id, ("gather", "tensor", partial_rows))[0], axis=0)


def dot_f32(left, right, left_dim, right_dim):
    return lax.dot_general(
        left, right, (((left_dim,), (right_dim,)), ((), ())), preferred_element_type=jnp.float32
    )


def per_device(
    tokens, cond, latent_count, cotangent, ada_w, ada_b, qkv_w, qv_b,
    out_w, out_b, fc1_w, fc1_b, fc2_w, fc2_b,
):
    latents, span, width = tokens.shape
    heads, head_size = qkv_w.shape[3], qkv_w.shape[4]
    inner = heads * head_size
    hidden = fc1_w.shape[2]
    shard_rows = qkv_w.shape[1]
    dp_size, ctx_size = lax.axis_size("dp"), lax.axis_size("ctx")
    rows = latents * span
    part = shard_rows // ctx_size
    f32 = lambda v: v.astype(jnp.float32)
    low = lambda v: v.astype(jnp.bfloat16)

    shard = jnp.concatenate(
        [qkv_w[0].reshape(shard_rows, 3 * inner), out_w[0].reshape(inner, shard_rows).T, fc1_w[0], fc2_w[0].T],
        axis=1,
    )
    columns = shard.shape[1]
    cond_float = f32(cond)
    silu_low = f32(low(jax.nn.silu(cond_float)))
    weights_all, silu_all = gather_weights(0, shard.reshape(ctx_size, part, columns), silu_low)
    weights_all = weights_all.reshape(width, columns)
    silu_all = silu_all.reshape(dp_size * latents, width)
    qkv_full = weights_all[:, : 3 * inner]
    out_t = weights_all[:, 3 * inner : 4 * inner]
    fc1_full = weights_all[:, 4 * inner : 4 * inner + hidden]
    fc2_t = weights_all[:, 4 * inner + hidden :]

    my_start = lax.axis_index("dp") * shard_rows
    silu_part = lax.dynamic_slice(silu_all, (0, my_start), (dp_size * latents, shard_rows))
    mod_part = dot_f32(low(silu_part), ada_w[0], 1, 0)
    (mod_parts,) = exchange(1, ("scatter", "dp", mod_part.reshape(dp_size, latents, 6 * width)))
    modulation = jnp.sum(mod_parts, axis=0) + f32(ada_b[0])
    shift_attn, scale_attn, gate_attn, shift_mlp, scale_mlp, gate_mlp = split_six(modulation, width)
    live_mask = f32(jnp.arange(latents) < latent_count[0])[:, None, None]

    stream = f32(tokens)
    normed_attn, inv_attn = layer_norm(stream)
    attn_in = low(normed_attn * (1.0 + scale_attn) + shift_attn).reshape(rows, width)
    bias_pair = f32(qv_b[0]).reshape(2, inner)
    bias_row = jnp.concatenate([bias_pair[0], jnp.zeros_like(bias_pair[0]), bias_pair[1]])
    qkv_rows = low(dot_f32(attn_in, qkv_full, 1, 0) + bias_row)
    queries = qkv_rows[:, :inner].reshape(latents, span, heads, head_size)
    (pairs,) = exchange(2, ("gather", "ctx", qkv_rows[:, inner:]))
    pairs = pairs.reshape(ctx_size, latents, span, 2, heads, head_size)
    pairs = jnp.transpose(pairs, (3, 1, 4, 0, 2, 5)).reshape(
        2, latents, heads, ctx_size * span, head_size
    )
    key_rows, value_rows = pairs[0], pairs[1]
    queries = jnp.transpose(queries, (0, 2, 1, 3))
    scale = float(HD) ** (-0.5)

    def batched(equation, left, right):
        return jnp.einsum(equation, left, right, preferred_element_type=jnp.float32)

    scores = batched("lhqe,lhke->lhqk", queries, key_rows) * scale
    weights = jnp.exp(scores - jnp.max(scores, axis=-1, keepdims=True))
    row_sum = jnp.sum(weights, axis=-1, keepdims=True)
    weights_low = low(weights)
    attended = batched("lhqk,lhke->lhqe", weights_low, value_rows) / row_sum
    attended_low = jnp.transpose(low(attended), (0, 2, 1, 3)).reshape(rows, inner)
    branch_attn = (
        tensor_total(3, dot_f32(attended_low, out_t, 1, 1)) + f32(out_b[0])
    ).reshape(latents, span, width)
    middle = stream + gate_attn * branch_attn
    normed_mlp, inv_mlp = layer_norm(middle)
    mlp_in = low(normed_mlp * (1.0 + scale_mlp) + shift_mlp).reshape(rows, width)
    hidden_pre = dot_f32(mlp_in, fc1_full, 1, 0) + f32(fc1_b[0])
    gelu_out, gelu_pull = jax.vjp(lambda point: jax.nn.gelu(point, approximate=True), hidden_pre)
    hidden_act = low(gelu_out)
    stream_grad = f32(cotangent) * live_mask
    mlp_grad = low(stream_grad * gate_mlp).reshape(rows, width)
    pre_grad = low(gelu_pull(dot_f32(mlp_grad, fc2_t, 1, 0))[0])
    both = exchange(
        4,
        ("gather", "tensor", dot_f32(hidden_act, fc2_t, 1, 1)),
        ("gather", "tensor", dot_f32(pre_grad, fc1_full, 1, 1)),
    )
    branch_mlp = (jnp.sum(both[0], axis=0) + f32(fc2_b[0])).reshape(latents, span, width)
    mlp_in_grad = jnp.sum(both[1], axis=0).reshape(latents, span, width)
    mixed = low((middle + gate_mlp * branch_mlp) * live_mask)
    gate_mlp_grad = jnp.sum(stream_grad * branch_mlp, axis=1)
    fc2_b_grad = jnp.sum(f32(mlp_grad), axis=0)
    fc2_grad_t = dot_f32(mlp_grad, hidden_act, 0, 0)
    fc1_b_grad = jnp.sum(f32(pre_grad), axis=0)
    fc1_grad = dot_f32(mlp_in, pre_grad, 0, 0)
    shift_mlp_grad = jnp.sum(mlp_in_grad, axis=1)
    scale_mlp_grad = jnp.sum(mlp_in_grad * normed_mlp, axis=1)
    middle_grad = stream_grad + norm_back(mlp_in_grad * (1.0 + scale_mlp), normed_mlp, inv_mlp)
    gate_attn_grad = jnp.sum(middle_grad * branch_attn, axis=1)
    branch_grad = low(middle_grad * gate_attn).reshape(rows, width)
    out_b_grad = jnp.sum(f32(branch_grad), axis=0)
    out_grad_t = dot_f32(branch_grad, attended_low, 0, 0)
    attn_grad = low(dot_f32(branch_grad, out_t, 1, 0)).reshape(latents, span, heads, head_size)
    attn_grad = jnp.transpose(attn_grad, (0, 2, 1, 3))
    delta = jnp.sum(f32(attn_grad) * attended, axis=-1, keepdims=True)
    prob_grad = batched("lhqe,lhke->lhqk", attn_grad, value_rows)
    score_grad = low(weights / row_sum * (prob_grad - delta))
    query_grad = low(scale * batched("lhqk,lhke->lhqe", score_grad, key_rows))
    key_grad = scale * batched("lhqk,lhqe->lhke", score_grad, queries)
    value_grad = batched("lhqk,lhqe->lhke", weights_low, low(f32(attn_grad) / row_sum))
    pair_grad = low(jnp.stack([key_grad, value_grad])).reshape(
        2, latents, heads, ctx_size, span, head_size
    )
    pair_grad = jnp.transpose(pair_grad, (3, 1, 4, 0, 2, 5)).reshape(ctx_size, rows, 2 * inner)
    (pair_parts,) = exchange(5, ("scatter", "ctx", pair_grad))
    pair_own = low(jnp.sum(f32(pair_parts), axis=0))
    flat_qkv = jnp.concatenate(
        [jnp.transpose(query_grad, (0, 2, 1, 3)).reshape(rows, inner), pair_own], axis=1
    )
    qkv_sums = jnp.sum(f32(flat_qkv), axis=0)
    qkv_grad = dot_f32(attn_in, flat_qkv, 0, 0)
    attn_in_grad = tensor_total(6, dot_f32(flat_qkv, qkv_full, 1, 1)).reshape(latents, span, width)
    shift_attn_grad = jnp.sum(attn_in_grad, axis=1)
    scale_attn_grad = jnp.sum(attn_in_grad * normed_attn, axis=1)
    tokens_grad = middle_grad + norm_back(attn_in_grad * (1.0 + scale_attn), normed_attn, inv_attn)
    mod_grad = jnp.concatenate(
        [shift_attn_grad, scale_attn_grad, gate_attn_grad, shift_mlp_grad, scale_mlp_grad, gate_mlp_grad],
        axis=1,
    )
    biases = jnp.concatenate(
        [qkv_sums[:inner], qkv_sums[2 * inner :], out_b_grad, fc1_b_grad, fc2_b_grad]
    )[None]

    all_grads = low(jnp.concatenate([qkv_grad, out_grad_t, fc1_grad, fc2_grad_t], axis=1))
    all_grads = jnp.transpose(all_grads.reshape(dp_size, ctx_size, part, columns), (1, 0, 2, 3))
    grad_parts, mod_parts, bias_parts = exchange(
        7, ("scatter", "ctx", all_grads), ("gather", "ctx", mod_grad), ("gather", "ctx", biases)
    )
    grad_part = low(jnp.sum(f32(grad_parts), axis=0))
    grad_parts, mod_all, bias_parts = exchange(
        8,
        ("scatter", "dp", grad_part),
        ("gather", "dp", jnp.sum(mod_parts, axis=0)),
        ("gather", "dp", jnp.sum(bias_parts, axis=0)),
    )
    grad_own = low(jnp.sum(f32(grad_parts), axis=0))
    bias_total = jnp.sum(bias_parts, axis=0)[0]
    mod_all = mod_all.reshape(dp_size * latents, 6 * width)
    ada_b_grad = jnp.sum(mod_all, axis=0)
    ada_w_grad = jnp.dot(silu_part.T, mod_all, precision=PRECISE)
    silu_grad = jnp.dot(mod_all, f32(ada_w[0]).T, precision=PRECISE)
    grads, silu_parts = exchange(
        9,
        ("gather", "ctx", grad_own),
        ("scatter", "dp", silu_grad.reshape(dp_size, latents, shard_rows)),
    )
    grads = f32(grads.reshape(shard_rows, columns))
    silu_total = jnp.transpose(silu_parts, (1, 0, 2)).reshape(latents, width)
    cond_grad = jax.vjp(jax.nn.silu, cond_float)[1](silu_total)[0]
    ends = [2 * inner, 2 * inner + width, 2 * inner + width + hidden]
    return (
        mixed,
        tokens_grad,
        cond_grad,
        ada_w_grad[None],
        ada_b_grad[None],
        grads[:, : 3 * inner].reshape(1, shard_rows, 3, heads, head_size),
        bias_total[: ends[0]].reshape(1, 2, heads, head_size),
        grads[:, 3 * inner : 4 * inner].T.reshape(1, heads, head_size, shard_rows),
        bias_total[ends[0] : ends[1]][None],
        grads[:, 4 * inner : 4 * inner + hidden][None],
        bias_total[ends[1] : ends[2]][None],
        grads[:, 4 * inner + hidden :].T[None],
        bias_total[ends[2] :][None],
    )


def solution(mesh):
    return jax.shard_map(
        per_device,
        mesh=mesh,
        in_specs=(
            P("dp", "ctx", None),
            P("dp", None),
            P("dp"),
            P("dp", "ctx", None),
            P(None, "dp", None),
            P(),
            P(None, "dp", None, "tensor", None),
            P(None, None, "tensor", None),
            P(None, "tensor", None, "dp"),
            P(),
            P(None, "dp", "tensor"),
            P(None, "tensor"),
            P(None, "tensor", "dp"),
            P(),
        ),
        out_specs=(
            P("dp", "ctx", None),
            P("dp", "ctx", None),
            P("dp", None),
            P(None, "dp", None),
            P(),
            P(None, "dp", None, "tensor", None),
            P(None, None, "tensor", None),
            P(None, "tensor", None, "dp"),
            P(),
            P(None, "dp", "tensor"),
            P(None, "tensor"),
            P(None, "tensor", "dp"),
            P(),
        ),
        check_vma=False,
    )
```

```python
import jax
import jax.numpy as jnp
from jax import lax
from jax.experimental import pallas as pl
from jax.experimental.pallas import tpu as pltpu
from jax.sharding import PartitionSpec as P

HD = 64


EPSILON = 1e-06
PRECISE = lax.Precision.HIGHEST


def layer_norm(residual_state):
    row_mean = jnp.mean(residual_state, axis=-1, keepdims=True)
    centered = residual_state - row_mean
    inv_std = lax.rsqrt(jnp.mean(centered * centered, axis=-1, keepdims=True) + EPSILON)
    return (centered * inv_std, inv_std)


def norm_back(upstream, normed, inv_std):
    first = jnp.mean(upstream, axis=-1, keepdims=True)
    second = jnp.mean(upstream * normed, axis=-1, keepdims=True)
    return inv_std * (upstream - first - normed * second)


def split_six(modulation, model_width):
    shaped = modulation.reshape(modulation.shape[0], 6, model_width)
    return [shaped[:, slot_index][:, None, :] for slot_index in range(6)]


MESH = pl.DeviceIdType.MESH
VMEM = pl.BlockSpec(memory_space=pltpu.VMEM)


def peer(axis, step):
    size = lax.axis_size(axis)
    return lax.rem(lax.axis_index(axis) + step, size)


def source(axis, step):
    size = lax.axis_size(axis)
    return lax.rem(lax.axis_index(axis) + size - step, size)


def greet(axes):
    barrier = pltpu.get_barrier_semaphore()
    total = 0
    for axis in axes:
        for step in range(1, lax.axis_size(axis)):
            pl.semaphore_signal(
                barrier, inc=1, device_id={axis: peer(axis, step)}, device_id_type=MESH
            )
            total += 1
    pl.semaphore_wait(barrier, total)


def exchange(collective_id, *items):
    count = len(items)
    axes = sorted({axis for _, axis, _ in items})
    steps_of = [lax.axis_size(axis) - 1 for _, axis, _ in items]
    firsts = [sum(steps_of[:which]) for which in range(count)]
    total = sum(steps_of)
    spread = [kind in ("gather", "total") for kind, _, _ in items]
    summed = [kind in ("total", "reduce") for kind, _, _ in items]
    landed = [
        (lax.axis_size(axis),) + (array.shape if spread[which] else array.shape[1:])
        for which, (_, axis, array) in enumerate(items)
    ]

    def body(*refs):
        ins, outs, rest = refs[:count], refs[count : 2 * count], list(refs[2 * count :])
        send_sem, recv_sem = rest.pop(0), rest.pop(0)
        slots = [rest.pop(0) if summed[which] else outs[which] for which in range(count)]
        greet(axes)
        copies = []
        for which, (_, axis, _) in enumerate(items):
            me = lax.axis_index(axis)
            for step in range(1, lax.axis_size(axis)):
                to = peer(axis, step)
                copy = pltpu.make_async_remote_copy(
                    src_ref=ins[which] if spread[which] else ins[which].at[to],
                    dst_ref=slots[which].at[me],
                    send_sem=send_sem.at[firsts[which] + step - 1],
                    recv_sem=recv_sem.at[firsts[which] + step - 1],
                    device_id={axis: to},
                    device_id_type=MESH,
                )
                copy.start()
                copies.append(copy)
        for which, (_, axis, _) in enumerate(items):
            me = lax.axis_index(axis)
            slots[which][me] = ins[which][...] if spread[which] else ins[which][me]
        for copy in copies:
            copy.wait()
        for which, (_, axis, _) in enumerate(items):
            if summed[which]:
                value = slots[which][0].astype(jnp.float32)
                for index in range(1, lax.axis_size(axis)):
                    value += slots[which][index].astype(jnp.float32)
                outs[which][...] = value.astype(outs[which].dtype)

    shapes = [
        jax.ShapeDtypeStruct(landed[which][1:] if summed[which] else landed[which], array.dtype)
        for which, (_, _, array) in enumerate(items)
    ]
    return pl.pallas_call(
        body,
        out_shape=shapes,
        in_specs=[VMEM] * count,
        out_specs=[VMEM] * count,
        scratch_shapes=[pltpu.SemaphoreType.DMA((total,)), pltpu.SemaphoreType.DMA((total,))]
        + [
            pltpu.VMEM(landed[which], array.dtype)
            for which, (_, _, array) in enumerate(items)
            if summed[which]
        ],
        compiler_params=pltpu.CompilerParams(
            collective_id=collective_id, has_side_effects=True, vmem_limit_bytes=50 << 20
        ),
        name="exchange",
    )(*[array for _, _, array in items])


def gather_weights(collective_id, shard, cond_rows):
    dp_size, ctx_size = lax.axis_size("dp"), lax.axis_size("ctx")
    far, near = dp_size - 1, ctx_size - 1

    def body(x, c, out, c_out, send_a, recv_a, send_b, recv_b, send_c, recv_c):
        row, col = lax.axis_index("dp"), lax.axis_index("ctx")
        greet(("dp", "ctx"))
        first, conds, later = [], [], []
        for step in range(1, dp_size):
            target = {"dp": peer("dp", step)}
            copy = pltpu.make_async_remote_copy(
                c, c_out.at[row], send_c.at[step - 1], recv_c.at[step - 1], target, MESH
            )
            copy.start()
            conds.append(copy)
            copy = pltpu.make_async_remote_copy(
                x.at[col], out.at[row, col], send_a.at[step - 1], recv_a.at[step - 1], target, MESH
            )
            copy.start()
            first.append(copy)
        out[row] = x[...]
        c_out[row] = c[...]
        for step in range(1, dp_size):
            first[step - 1].wait_recv()
            origin = source("dp", step)
            for hop in range(1, ctx_size):
                where = (step - 1) * near + hop - 1
                copy = pltpu.make_async_remote_copy(
                    out.at[origin, col],
                    out.at[origin, col],
                    send_b.at[where],
                    recv_b.at[where],
                    {"ctx": peer("ctx", hop)},
                    MESH,
                )
                copy.start()
                later.append(copy)
        for copy in first:
            copy.wait_send()
        for copy in conds + later:
            copy.wait()

    dma = pltpu.SemaphoreType.DMA
    return pl.pallas_call(
        body,
        out_shape=[
            jax.ShapeDtypeStruct((dp_size,) + shard.shape, shard.dtype),
            jax.ShapeDtypeStruct((dp_size,) + cond_rows.shape, cond_rows.dtype),
        ],
        in_specs=[VMEM] * 2,
        out_specs=[VMEM] * 2,
        scratch_shapes=[
            dma((far,)),
            dma((far,)),
            dma((far * near,)),
            dma((far * near,)),
            dma((far,)),
            dma((far,)),
        ],
        compiler_params=pltpu.CompilerParams(
            collective_id=collective_id, has_side_effects=True, vmem_limit_bytes=50 << 20
        ),
        name="gather_weights",
    )(shard, cond_rows)


def tensor_total(collective_id, partial_rows):
    return exchange(collective_id, ("total", "tensor", partial_rows))[0]


def dot_f32(left, right, left_dim, right_dim):
    return lax.dot_general(
        left, right, (((left_dim,), (right_dim,)), ((), ())), preferred_element_type=jnp.float32
    )


def per_device(
    tokens, cond, latent_count, cotangent, ada_w, ada_b, qkv_w, qv_b,
    out_w, out_b, fc1_w, fc1_b, fc2_w, fc2_b,
):
    latents, span, width = tokens.shape
    heads, head_size = qkv_w.shape[3], qkv_w.shape[4]
    inner = heads * head_size
    hidden = fc1_w.shape[2]
    shard_rows = qkv_w.shape[1]
    dp_size, ctx_size = lax.axis_size("dp"), lax.axis_size("ctx")
    rows = latents * span
    part = shard_rows // ctx_size
    f32 = lambda v: v.astype(jnp.float32)
    low = lambda v: v.astype(jnp.bfloat16)

    shard = jnp.concatenate(
        [qkv_w[0].reshape(shard_rows, 3 * inner), out_w[0].reshape(inner, shard_rows).T, fc1_w[0], fc2_w[0].T],
        axis=1,
    )
    columns = shard.shape[1]
    cond_float = f32(cond)
    silu_low = f32(low(jax.nn.silu(cond_float)))
    weights_all, silu_all = gather_weights(0, shard.reshape(ctx_size, part, columns), silu_low)
    weights_all = weights_all.reshape(width, columns)
    silu_all = silu_all.reshape(dp_size * latents, width)
    qkv_full = weights_all[:, : 3 * inner]
    out_t = weights_all[:, 3 * inner : 4 * inner]
    fc1_full = weights_all[:, 4 * inner : 4 * inner + hidden]
    fc2_t = weights_all[:, 4 * inner + hidden :]

    my_start = lax.axis_index("dp") * shard_rows
    silu_part = lax.dynamic_slice(silu_all, (0, my_start), (dp_size * latents, shard_rows))
    mod_part = dot_f32(low(silu_part), ada_w[0], 1, 0)
    (mod_sum,) = exchange(1, ("reduce", "dp", mod_part.reshape(dp_size, latents, 6 * width)))
    modulation = mod_sum + f32(ada_b[0])
    shift_attn, scale_attn, gate_attn, shift_mlp, scale_mlp, gate_mlp = split_six(modulation, width)
    live_mask = f32(jnp.arange(latents) < latent_count[0])[:, None, None]

    stream = f32(tokens)
    normed_attn, inv_attn = layer_norm(stream)
    attn_in = low(normed_attn * (1.0 + scale_attn) + shift_attn).reshape(rows, width)
    bias_pair = f32(qv_b[0]).reshape(2, inner)
    bias_row = jnp.concatenate([bias_pair[0], jnp.zeros_like(bias_pair[0]), bias_pair[1]])
    qkv_rows = low(dot_f32(attn_in, qkv_full, 1, 0) + bias_row)
    queries = qkv_rows[:, :inner].reshape(latents, span, heads, head_size)
    (pairs,) = exchange(2, ("gather", "ctx", qkv_rows[:, inner:]))
    pairs = pairs.reshape(ctx_size, latents, span, 2, heads, head_size)
    pairs = jnp.transpose(pairs, (3, 1, 4, 0, 2, 5)).reshape(
        2, latents, heads, ctx_size * span, head_size
    )
    key_rows, value_rows = pairs[0], pairs[1]
    queries = jnp.transpose(queries, (0, 2, 1, 3))
    scale = float(HD) ** (-0.5)

    def batched(equation, left, right):
        return jnp.einsum(equation, left, right, preferred_element_type=jnp.float32)

    scores = batched("lhqe,lhke->lhqk", queries, key_rows) * scale
    weights = jnp.exp(scores - jnp.max(scores, axis=-1, keepdims=True))
    row_sum = jnp.sum(weights, axis=-1, keepdims=True)
    weights_low = low(weights)
    attended = batched("lhqk,lhke->lhqe", weights_low, value_rows) / row_sum
    attended_low = jnp.transpose(low(attended), (0, 2, 1, 3)).reshape(rows, inner)
    branch_attn = (
        tensor_total(3, dot_f32(attended_low, out_t, 1, 1)) + f32(out_b[0])
    ).reshape(latents, span, width)
    middle = stream + gate_attn * branch_attn
    normed_mlp, inv_mlp = layer_norm(middle)
    mlp_in = low(normed_mlp * (1.0 + scale_mlp) + shift_mlp).reshape(rows, width)
    hidden_pre = dot_f32(mlp_in, fc1_full, 1, 0) + f32(fc1_b[0])
    gelu_out, gelu_pull = jax.vjp(lambda point: jax.nn.gelu(point, approximate=True), hidden_pre)
    hidden_act = low(gelu_out)
    stream_grad = f32(cotangent) * live_mask
    mlp_grad = low(stream_grad * gate_mlp).reshape(rows, width)
    pre_grad = low(gelu_pull(dot_f32(mlp_grad, fc2_t, 1, 0))[0])
    both = exchange(
        4,
        ("total", "tensor", dot_f32(hidden_act, fc2_t, 1, 1)),
        ("total", "tensor", dot_f32(pre_grad, fc1_full, 1, 1)),
    )
    branch_mlp = (both[0] + f32(fc2_b[0])).reshape(latents, span, width)
    mlp_in_grad = both[1].reshape(latents, span, width)
    mixed = low((middle + gate_mlp * branch_mlp) * live_mask)
    gate_mlp_grad = jnp.sum(stream_grad * branch_mlp, axis=1)
    fc2_b_grad = jnp.sum(f32(mlp_grad), axis=0)
    fc2_grad_t = dot_f32(mlp_grad, hidden_act, 0, 0)
    fc1_b_grad = jnp.sum(f32(pre_grad), axis=0)
    fc1_grad = dot_f32(mlp_in, pre_grad, 0, 0)
    shift_mlp_grad = jnp.sum(mlp_in_grad, axis=1)
    scale_mlp_grad = jnp.sum(mlp_in_grad * normed_mlp, axis=1)
    middle_grad = stream_grad + norm_back(mlp_in_grad * (1.0 + scale_mlp), normed_mlp, inv_mlp)
    gate_attn_grad = jnp.sum(middle_grad * branch_attn, axis=1)
    branch_grad = low(middle_grad * gate_attn).reshape(rows, width)
    out_b_grad = jnp.sum(f32(branch_grad), axis=0)
    out_grad_t = dot_f32(branch_grad, attended_low, 0, 0)
    attn_grad = low(dot_f32(branch_grad, out_t, 1, 0)).reshape(latents, span, heads, head_size)
    attn_grad = jnp.transpose(attn_grad, (0, 2, 1, 3))
    delta = jnp.sum(f32(attn_grad) * attended, axis=-1, keepdims=True)
    prob_grad = batched("lhqe,lhke->lhqk", attn_grad, value_rows)
    score_grad = low(weights / row_sum * (prob_grad - delta))
    query_grad = low(scale * batched("lhqk,lhke->lhqe", score_grad, key_rows))
    key_grad = scale * batched("lhqk,lhqe->lhke", score_grad, queries)
    value_grad = batched("lhqk,lhqe->lhke", weights_low, low(f32(attn_grad) / row_sum))
    pair_grad = low(jnp.stack([key_grad, value_grad])).reshape(
        2, latents, heads, ctx_size, span, head_size
    )
    pair_grad = jnp.transpose(pair_grad, (3, 1, 4, 0, 2, 5)).reshape(ctx_size, rows, 2 * inner)
    (pair_own,) = exchange(5, ("reduce", "ctx", pair_grad))
    flat_qkv = jnp.concatenate(
        [jnp.transpose(query_grad, (0, 2, 1, 3)).reshape(rows, inner), pair_own], axis=1
    )
    qkv_sums = jnp.sum(f32(flat_qkv), axis=0)
    qkv_grad = dot_f32(attn_in, flat_qkv, 0, 0)
    attn_in_grad = tensor_total(6, dot_f32(flat_qkv, qkv_full, 1, 1)).reshape(latents, span, width)
    shift_attn_grad = jnp.sum(attn_in_grad, axis=1)
    scale_attn_grad = jnp.sum(attn_in_grad * normed_attn, axis=1)
    tokens_grad = middle_grad + norm_back(attn_in_grad * (1.0 + scale_attn), normed_attn, inv_attn)
    mod_grad = jnp.concatenate(
        [shift_attn_grad, scale_attn_grad, gate_attn_grad, shift_mlp_grad, scale_mlp_grad, gate_mlp_grad],
        axis=1,
    )
    biases = jnp.concatenate(
        [qkv_sums[:inner], qkv_sums[2 * inner :], out_b_grad, fc1_b_grad, fc2_b_grad]
    )[None]

    all_grads = low(jnp.concatenate([qkv_grad, out_grad_t, fc1_grad, fc2_grad_t], axis=1))
    all_grads = jnp.transpose(all_grads.reshape(dp_size, ctx_size, part, columns), (1, 0, 2, 3)).reshape(
        ctx_size, dp_size * part, columns
    )
    grad_part, mod_sum, bias_sum = exchange(
        7, ("reduce", "ctx", all_grads), ("total", "ctx", mod_grad), ("total", "ctx", biases)
    )
    grad_own, mod_all, bias_total = exchange(
        8,
        ("reduce", "dp", grad_part.reshape(dp_size, part, columns)),
        ("gather", "dp", mod_sum),
        ("total", "dp", bias_sum),
    )
    bias_total = bias_total[0]
    mod_all = mod_all.reshape(dp_size * latents, 6 * width)
    ada_b_grad = jnp.sum(mod_all, axis=0)
    ada_w_grad = jnp.dot(silu_part.T, mod_all, precision=PRECISE)
    silu_grad = jnp.dot(mod_all, f32(ada_w[0]).T, precision=PRECISE)
    grads, silu_parts = exchange(
        9,
        ("gather", "ctx", grad_own),
        ("scatter", "dp", silu_grad.reshape(dp_size, latents, shard_rows)),
    )
    grads = f32(grads.reshape(shard_rows, columns))
    silu_total = jnp.transpose(silu_parts, (1, 0, 2)).reshape(latents, width)
    cond_grad = jax.vjp(jax.nn.silu, cond_float)[1](silu_total)[0]
    ends = [2 * inner, 2 * inner + width, 2 * inner + width + hidden]
    return (
        mixed,
        tokens_grad,
        cond_grad,
        ada_w_grad[None],
        ada_b_grad[None],
        grads[:, : 3 * inner].reshape(1, shard_rows, 3, heads, head_size),
        bias_total[: ends[0]].reshape(1, 2, heads, head_size),
        grads[:, 3 * inner : 4 * inner].T.reshape(1, heads, head_size, shard_rows),
        bias_total[ends[0] : ends[1]][None],
        grads[:, 4 * inner : 4 * inner + hidden][None],
        bias_total[ends[1] : ends[2]][None],
        grads[:, 4 * inner + hidden :].T[None],
        bias_total[ends[2] :][None],
    )


def solution(mesh):
    return jax.shard_map(
        per_device,
        mesh=mesh,
        in_specs=(
            P("dp", "ctx", None),
            P("dp", None),
            P("dp"),
            P("dp", "ctx", None),
            P(None, "dp", None),
            P(),
            P(None, "dp", None, "tensor", None),
            P(None, None, "tensor", None),
            P(None, "tensor", None, "dp"),
            P(),
            P(None, "dp", "tensor"),
            P(None, "tensor"),
            P(None, "tensor", "dp"),
            P(),
        ),
        out_specs=(
            P("dp", "ctx", None),
            P("dp", "ctx", None),
            P("dp", None),
            P(None, "dp", None),
            P(),
            P(None, "dp", None, "tensor", None),
            P(None, None, "tensor", None),
            P(None, "tensor", None, "dp"),
            P(),
            P(None, "dp", "tensor"),
            P(None, "tensor"),
            P(None, "tensor", "dp"),
            P(),
        ),
        check_vma=False,
    )
```

```python
import jax
import jax.numpy as jnp
from jax import lax
from jax.experimental import pallas as pl
from jax.experimental.pallas import tpu as pltpu
from jax.sharding import PartitionSpec as P

HD = 64


EPSILON = 1e-06
PRECISE = lax.Precision.HIGHEST


def layer_norm(residual_state):
    row_mean = jnp.mean(residual_state, axis=-1, keepdims=True)
    centered = residual_state - row_mean
    inv_std = lax.rsqrt(jnp.mean(centered * centered, axis=-1, keepdims=True) + EPSILON)
    return (centered * inv_std, inv_std)


def norm_back(upstream, normed, inv_std):
    first = jnp.mean(upstream, axis=-1, keepdims=True)
    second = jnp.mean(upstream * normed, axis=-1, keepdims=True)
    return inv_std * (upstream - first - normed * second)


def split_six(modulation, model_width):
    shaped = modulation.reshape(modulation.shape[0], 6, model_width)
    return [shaped[:, slot_index][:, None, :] for slot_index in range(6)]


MESH = pl.DeviceIdType.MESH
VMEM = pl.BlockSpec(memory_space=pltpu.VMEM)


def peer(axis, step):
    size = lax.axis_size(axis)
    return lax.rem(lax.axis_index(axis) + step, size)


def source(axis, step):
    size = lax.axis_size(axis)
    return lax.rem(lax.axis_index(axis) + size - step, size)


def greet(axes):
    barrier = pltpu.get_barrier_semaphore()
    total = 0
    for axis in axes:
        for step in range(1, lax.axis_size(axis)):
            pl.semaphore_signal(
                barrier, inc=1, device_id={axis: peer(axis, step)}, device_id_type=MESH
            )
            total += 1
    pl.semaphore_wait(barrier, total)


def exchange(collective_id, *items):
    count = len(items)
    axes = sorted({axis for _, axis, _ in items})
    steps_of = [lax.axis_size(axis) - 1 for _, axis, _ in items]
    firsts = [sum(steps_of[:which]) for which in range(count)]
    total = sum(steps_of)
    spread = [kind in ("gather", "total") for kind, _, _ in items]
    summed = [kind in ("total", "reduce") for kind, _, _ in items]
    landed = [
        (lax.axis_size(axis),) + (array.shape if spread[which] else array.shape[1:])
        for which, (_, axis, array) in enumerate(items)
    ]

    def body(*refs):
        ins, outs, rest = refs[:count], refs[count : 2 * count], list(refs[2 * count :])
        send_sem, recv_sem = rest.pop(0), rest.pop(0)
        slots = [rest.pop(0) if summed[which] else outs[which] for which in range(count)]
        greet(axes)
        copies = []
        for which, (_, axis, _) in enumerate(items):
            me = lax.axis_index(axis)
            for step in range(1, lax.axis_size(axis)):
                to = peer(axis, step)
                copy = pltpu.make_async_remote_copy(
                    src_ref=ins[which] if spread[which] else ins[which].at[to],
                    dst_ref=slots[which].at[me],
                    send_sem=send_sem.at[firsts[which] + step - 1],
                    recv_sem=recv_sem.at[firsts[which] + step - 1],
                    device_id={axis: to},
                    device_id_type=MESH,
                )
                copy.start()
                copies.append(copy)
        for which, (_, axis, _) in enumerate(items):
            me = lax.axis_index(axis)
            slots[which][me] = ins[which][...] if spread[which] else ins[which][me]
        for copy in copies:
            copy.wait()
        for which, (_, axis, _) in enumerate(items):
            if summed[which]:
                value = slots[which][0].astype(jnp.float32)
                for index in range(1, lax.axis_size(axis)):
                    value += slots[which][index].astype(jnp.float32)
                outs[which][...] = value.astype(outs[which].dtype)

    shapes = [
        jax.ShapeDtypeStruct(landed[which][1:] if summed[which] else landed[which], array.dtype)
        for which, (_, _, array) in enumerate(items)
    ]
    return pl.pallas_call(
        body,
        out_shape=shapes,
        in_specs=[VMEM] * count,
        out_specs=[VMEM] * count,
        scratch_shapes=[pltpu.SemaphoreType.DMA((total,)), pltpu.SemaphoreType.DMA((total,))]
        + [
            pltpu.VMEM(landed[which], array.dtype)
            for which, (_, _, array) in enumerate(items)
            if summed[which]
        ],
        compiler_params=pltpu.CompilerParams(
            collective_id=collective_id, has_side_effects=True, vmem_limit_bytes=50 << 20
        ),
        name="exchange",
    )(*[array for _, _, array in items])


def gather_weights(collective_id, shard, cond_rows):
    dp_size, ctx_size = lax.axis_size("dp"), lax.axis_size("ctx")
    far, near = dp_size - 1, ctx_size - 1

    def body(x, c, out, c_out, send_a, recv_a, send_b, recv_b, send_c, recv_c):
        row, col = lax.axis_index("dp"), lax.axis_index("ctx")
        greet(("dp", "ctx"))
        first, conds, later = [], [], []
        for step in range(1, dp_size):
            target = {"dp": peer("dp", step)}
            copy = pltpu.make_async_remote_copy(
                c, c_out.at[row], send_c.at[step - 1], recv_c.at[step - 1], target, MESH
            )
            copy.start()
            conds.append(copy)
            copy = pltpu.make_async_remote_copy(
                x.at[col], out.at[row, col], send_a.at[step - 1], recv_a.at[step - 1], target, MESH
            )
            copy.start()
            first.append(copy)
        out[row] = x[...]
        c_out[row] = c[...]
        for step in range(1, dp_size):
            first[step - 1].wait_recv()
            origin = source("dp", step)
            for hop in range(1, ctx_size):
                where = (step - 1) * near + hop - 1
                copy = pltpu.make_async_remote_copy(
                    out.at[origin, col],
                    out.at[origin, col],
                    send_b.at[where],
                    recv_b.at[where],
                    {"ctx": peer("ctx", hop)},
                    MESH,
                )
                copy.start()
                later.append(copy)
        for copy in first:
            copy.wait_send()
        for copy in conds + later:
            copy.wait()

    dma = pltpu.SemaphoreType.DMA
    return pl.pallas_call(
        body,
        out_shape=[
            jax.ShapeDtypeStruct((dp_size,) + shard.shape, shard.dtype),
            jax.ShapeDtypeStruct((dp_size,) + cond_rows.shape, cond_rows.dtype),
        ],
        in_specs=[VMEM] * 2,
        out_specs=[VMEM] * 2,
        scratch_shapes=[
            dma((far,)),
            dma((far,)),
            dma((far * near,)),
            dma((far * near,)),
            dma((far,)),
            dma((far,)),
        ],
        compiler_params=pltpu.CompilerParams(
            collective_id=collective_id, has_side_effects=True, vmem_limit_bytes=50 << 20
        ),
        name="gather_weights",
    )(shard, cond_rows)


def tensor_total(collective_id, partial_rows):
    return exchange(collective_id, ("total", "tensor", partial_rows))[0]


def dot_f32(left, right, left_dim, right_dim):
    return lax.dot_general(
        left, right, (((left_dim,), (right_dim,)), ((), ())), preferred_element_type=jnp.float32
    )


def attention_weights(queries, keys):
    scores = dot_f32(queries, keys, 1, 1) * float(HD) ** (-0.5)
    weights = jnp.exp(scores - jnp.max(scores, axis=-1, keepdims=True))
    return weights, jnp.sum(weights, axis=-1, keepdims=True)


def attention_blocks(latents, span, inner):
    for latent in range(latents):
        for start in range(0, inner, HD):
            yield slice(latent * span, (latent + 1) * span), start


def attention_forward(qkv_rows, pairs, latents):
    rows, inner = qkv_rows.shape[0], qkv_rows.shape[1] // 3
    span = rows // latents
    keys_total = pairs.shape[0] * span

    def body(q_ref, kv_ref, o_ref, low_ref):
        for here, start in attention_blocks(latents, span, inner):
            queries = q_ref[here, start : start + HD]
            keys = kv_ref[:, here, start : start + HD].reshape(keys_total, HD)
            values = kv_ref[:, here, inner + start : inner + start + HD].reshape(keys_total, HD)
            weights, row_sum = attention_weights(queries, keys)
            out = dot_f32(weights.astype(jnp.bfloat16), values, 1, 0) / row_sum
            o_ref[here, start : start + HD] = out
            low_ref[here, start : start + HD] = out.astype(jnp.bfloat16)

    return pl.pallas_call(
        body,
        out_shape=[
            jax.ShapeDtypeStruct((rows, inner), jnp.float32),
            jax.ShapeDtypeStruct((rows, inner), jnp.bfloat16),
        ],
        in_specs=[VMEM] * 2,
        out_specs=[VMEM] * 2,
        compiler_params=pltpu.CompilerParams(vmem_limit_bytes=50 << 20),
        name="attention_forward",
    )(qkv_rows, pairs)


def attention_backward(qkv_rows, pairs, attended, attn_grad, latents):
    rows, inner = attended.shape
    span = rows // latents
    ctx_size = pairs.shape[0]
    keys_total = ctx_size * span
    scale = float(HD) ** (-0.5)

    def body(q_ref, kv_ref, o_ref, g_ref, q_grad_ref, pair_ref):
        for here, start in attention_blocks(latents, span, inner):
            queries = q_ref[here, start : start + HD]
            keys = kv_ref[:, here, start : start + HD].reshape(keys_total, HD)
            values = kv_ref[:, here, inner + start : inner + start + HD].reshape(keys_total, HD)
            upstream = g_ref[here, start : start + HD]
            wide = upstream.astype(jnp.float32)
            weights, row_sum = attention_weights(queries, keys)
            delta = jnp.sum(wide * o_ref[here, start : start + HD], axis=-1, keepdims=True)
            prob_grad = dot_f32(upstream, values, 1, 1)
            score_grad = (weights / row_sum * (prob_grad - delta)).astype(jnp.bfloat16)
            q_grad_ref[here, start : start + HD] = (
                scale * dot_f32(score_grad, keys, 1, 0)
            ).astype(jnp.bfloat16)
            key_grad = (scale * dot_f32(score_grad, queries, 0, 0)).astype(jnp.bfloat16)
            value_grad = dot_f32(
                weights.astype(jnp.bfloat16), (wide / row_sum).astype(jnp.bfloat16), 0, 0
            ).astype(jnp.bfloat16)
            pair_ref[:, here, start : start + HD] = key_grad.reshape(ctx_size, span, HD)
            pair_ref[:, here, inner + start : inner + start + HD] = value_grad.reshape(
                ctx_size, span, HD
            )

    return pl.pallas_call(
        body,
        out_shape=[
            jax.ShapeDtypeStruct((rows, inner), jnp.bfloat16),
            jax.ShapeDtypeStruct(pairs.shape, jnp.bfloat16),
        ],
        in_specs=[VMEM] * 4,
        out_specs=[VMEM] * 2,
        compiler_params=pltpu.CompilerParams(vmem_limit_bytes=50 << 20),
        name="attention_backward",
    )(qkv_rows, pairs, attended, attn_grad)


def per_device(
    tokens, cond, latent_count, cotangent, ada_w, ada_b, qkv_w, qv_b,
    out_w, out_b, fc1_w, fc1_b, fc2_w, fc2_b,
):
    latents, span, width = tokens.shape
    heads, head_size = qkv_w.shape[3], qkv_w.shape[4]
    inner = heads * head_size
    hidden = fc1_w.shape[2]
    shard_rows = qkv_w.shape[1]
    dp_size, ctx_size = lax.axis_size("dp"), lax.axis_size("ctx")
    rows = latents * span
    part = shard_rows // ctx_size
    f32 = lambda v: v.astype(jnp.float32)
    low = lambda v: v.astype(jnp.bfloat16)

    shard = jnp.concatenate(
        [qkv_w[0].reshape(shard_rows, 3 * inner), out_w[0].reshape(inner, shard_rows).T, fc1_w[0], fc2_w[0].T],
        axis=1,
    )
    columns = shard.shape[1]
    cond_float = f32(cond)
    silu_low = f32(low(jax.nn.silu(cond_float)))
    weights_all, silu_all = gather_weights(0, shard.reshape(ctx_size, part, columns), silu_low)
    weights_all = weights_all.reshape(width, columns)
    silu_all = silu_all.reshape(dp_size * latents, width)
    qkv_full = weights_all[:, : 3 * inner]
    out_t = weights_all[:, 3 * inner : 4 * inner]
    fc1_full = weights_all[:, 4 * inner : 4 * inner + hidden]
    fc2_t = weights_all[:, 4 * inner + hidden :]

    my_start = lax.axis_index("dp") * shard_rows
    silu_part = lax.dynamic_slice(silu_all, (0, my_start), (dp_size * latents, shard_rows))
    mod_part = dot_f32(low(silu_part), ada_w[0], 1, 0)
    (mod_sum,) = exchange(1, ("reduce", "dp", mod_part.reshape(dp_size, latents, 6 * width)))
    modulation = mod_sum + f32(ada_b[0])
    shift_attn, scale_attn, gate_attn, shift_mlp, scale_mlp, gate_mlp = split_six(modulation, width)
    live_mask = f32(jnp.arange(latents) < latent_count[0])[:, None, None]

    stream = f32(tokens)
    normed_attn, inv_attn = layer_norm(stream)
    attn_in = low(normed_attn * (1.0 + scale_attn) + shift_attn).reshape(rows, width)
    bias_pair = f32(qv_b[0]).reshape(2, inner)
    bias_row = jnp.concatenate([bias_pair[0], jnp.zeros_like(bias_pair[0]), bias_pair[1]])
    qkv_rows = low(dot_f32(attn_in, qkv_full, 1, 0) + bias_row)
    (pairs,) = exchange(2, ("gather", "ctx", qkv_rows[:, inner:]))
    attended, attended_low = attention_forward(qkv_rows, pairs, latents)
    branch_attn = (
        tensor_total(3, dot_f32(attended_low, out_t, 1, 1)) + f32(out_b[0])
    ).reshape(latents, span, width)
    middle = stream + gate_attn * branch_attn
    normed_mlp, inv_mlp = layer_norm(middle)
    mlp_in = low(normed_mlp * (1.0 + scale_mlp) + shift_mlp).reshape(rows, width)
    hidden_pre = dot_f32(mlp_in, fc1_full, 1, 0) + f32(fc1_b[0])
    gelu_out, gelu_pull = jax.vjp(lambda point: jax.nn.gelu(point, approximate=True), hidden_pre)
    hidden_act = low(gelu_out)
    stream_grad = f32(cotangent) * live_mask
    mlp_grad = low(stream_grad * gate_mlp).reshape(rows, width)
    pre_grad = low(gelu_pull(dot_f32(mlp_grad, fc2_t, 1, 0))[0])
    both = exchange(
        4,
        ("total", "tensor", dot_f32(hidden_act, fc2_t, 1, 1)),
        ("total", "tensor", dot_f32(pre_grad, fc1_full, 1, 1)),
    )
    branch_mlp = (both[0] + f32(fc2_b[0])).reshape(latents, span, width)
    mlp_in_grad = both[1].reshape(latents, span, width)
    mixed = low((middle + gate_mlp * branch_mlp) * live_mask)
    gate_mlp_grad = jnp.sum(stream_grad * branch_mlp, axis=1)
    fc2_b_grad = jnp.sum(f32(mlp_grad), axis=0)
    fc2_grad_t = dot_f32(mlp_grad, hidden_act, 0, 0)
    fc1_b_grad = jnp.sum(f32(pre_grad), axis=0)
    fc1_grad = dot_f32(mlp_in, pre_grad, 0, 0)
    shift_mlp_grad = jnp.sum(mlp_in_grad, axis=1)
    scale_mlp_grad = jnp.sum(mlp_in_grad * normed_mlp, axis=1)
    middle_grad = stream_grad + norm_back(mlp_in_grad * (1.0 + scale_mlp), normed_mlp, inv_mlp)
    gate_attn_grad = jnp.sum(middle_grad * branch_attn, axis=1)
    branch_grad = low(middle_grad * gate_attn).reshape(rows, width)
    out_b_grad = jnp.sum(f32(branch_grad), axis=0)
    out_grad_t = dot_f32(branch_grad, attended_low, 0, 0)
    attn_grad = low(dot_f32(branch_grad, out_t, 1, 0))
    query_grad, pair_grad = attention_backward(qkv_rows, pairs, attended, attn_grad, latents)
    (pair_own,) = exchange(5, ("reduce", "ctx", pair_grad))
    flat_qkv = jnp.concatenate([query_grad, pair_own], axis=1)
    qkv_sums = jnp.sum(f32(flat_qkv), axis=0)
    qkv_grad = dot_f32(attn_in, flat_qkv, 0, 0)
    attn_in_grad = tensor_total(6, dot_f32(flat_qkv, qkv_full, 1, 1)).reshape(latents, span, width)
    shift_attn_grad = jnp.sum(attn_in_grad, axis=1)
    scale_attn_grad = jnp.sum(attn_in_grad * normed_attn, axis=1)
    tokens_grad = middle_grad + norm_back(attn_in_grad * (1.0 + scale_attn), normed_attn, inv_attn)
    mod_grad = jnp.concatenate(
        [shift_attn_grad, scale_attn_grad, gate_attn_grad, shift_mlp_grad, scale_mlp_grad, gate_mlp_grad],
        axis=1,
    )
    biases = jnp.concatenate(
        [qkv_sums[:inner], qkv_sums[2 * inner :], out_b_grad, fc1_b_grad, fc2_b_grad]
    )[None]

    all_grads = low(jnp.concatenate([qkv_grad, out_grad_t, fc1_grad, fc2_grad_t], axis=1))
    all_grads = jnp.transpose(all_grads.reshape(dp_size, ctx_size, part, columns), (1, 0, 2, 3)).reshape(
        ctx_size, dp_size * part, columns
    )
    grad_part, mod_sum, bias_sum = exchange(
        7, ("reduce", "ctx", all_grads), ("total", "ctx", mod_grad), ("total", "ctx", biases)
    )
    grad_own, mod_all, bias_total = exchange(
        8,
        ("reduce", "dp", grad_part.reshape(dp_size, part, columns)),
        ("gather", "dp", mod_sum),
        ("total", "dp", bias_sum),
    )
    bias_total = bias_total[0]
    mod_all = mod_all.reshape(dp_size * latents, 6 * width)
    ada_b_grad = jnp.sum(mod_all, axis=0)
    ada_w_grad = jnp.dot(silu_part.T, mod_all, precision=PRECISE)
    silu_grad = jnp.dot(mod_all, f32(ada_w[0]).T, precision=PRECISE)
    grads, silu_parts = exchange(
        9,
        ("gather", "ctx", grad_own),
        ("scatter", "dp", silu_grad.reshape(dp_size, latents, shard_rows)),
    )
    grads = f32(grads.reshape(shard_rows, columns))
    silu_total = jnp.transpose(silu_parts, (1, 0, 2)).reshape(latents, width)
    cond_grad = jax.vjp(jax.nn.silu, cond_float)[1](silu_total)[0]
    ends = [2 * inner, 2 * inner + width, 2 * inner + width + hidden]
    return (
        mixed,
        tokens_grad,
        cond_grad,
        ada_w_grad[None],
        ada_b_grad[None],
        grads[:, : 3 * inner].reshape(1, shard_rows, 3, heads, head_size),
        bias_total[: ends[0]].reshape(1, 2, heads, head_size),
        grads[:, 3 * inner : 4 * inner].T.reshape(1, heads, head_size, shard_rows),
        bias_total[ends[0] : ends[1]][None],
        grads[:, 4 * inner : 4 * inner + hidden][None],
        bias_total[ends[1] : ends[2]][None],
        grads[:, 4 * inner + hidden :].T[None],
        bias_total[ends[2] :][None],
    )


def solution(mesh):
    return jax.shard_map(
        per_device,
        mesh=mesh,
        in_specs=(
            P("dp", "ctx", None),
            P("dp", None),
            P("dp"),
            P("dp", "ctx", None),
            P(None, "dp", None),
            P(),
            P(None, "dp", None, "tensor", None),
            P(None, None, "tensor", None),
            P(None, "tensor", None, "dp"),
            P(),
            P(None, "dp", "tensor"),
            P(None, "tensor"),
            P(None, "tensor", "dp"),
            P(),
        ),
        out_specs=(
            P("dp", "ctx", None),
            P("dp", "ctx", None),
            P("dp", None),
            P(None, "dp", None),
            P(),
            P(None, "dp", None, "tensor", None),
            P(None, None, "tensor", None),
            P(None, "tensor", None, "dp"),
            P(),
            P(None, "dp", "tensor"),
            P(None, "tensor"),
            P(None, "tensor", "dp"),
            P(),
        ),
        check_vma=False,
    )
```
